128 devices in a mesh: row: 16 (over z, x_lo, core), col: 8 (over y, x_hi).
Axes of the slice: x: 4 (x_hi: 2, x_lo: 2; x = x_hi * 2 + x_lo), y: 4, z: 4, core: 2. Of those that a mesh axis runs over, the one named last changes fastest.
Arguments:
- tokens: bfloat16 [1024, 12288], P('col', 'row'), may hold values from -6 to 6
- weight_in: bfloat16 [12288, 24576], P('row', 'col'), may hold values from -0.0546875 to 0.0546875
- weight_out: bfloat16 [24576, 12288], P('col', 'row'), may hold values from -0.0390625 to 0.0390625
- bias_in: bfloat16 [24576], P('col'), may hold values from -3 to 3
- cotangent: bfloat16 [1024, 12288], P('col', 'row'), may hold values from -6 to 6
Outputs:
- output: bfloat16 [1024, 12288], P('col', 'row')
- grad_tokens: bfloat16 [1024, 12288], P('col', 'row')
- grad_weight_in: bfloat16 [12288, 24576], P('row', 'col')
- grad_weight_out: bfloat16 [24576, 12288], P('col', 'row')
- grad_bias: float32 [24576], P('col')
The draws below stay inside these ranges and needn't reach their ends.
All inputs are finite; a program needn't handle non-finite values.
Results may differ from the reference program's by a relative error of at most 0.03.
Values may be sent and summed in bfloat16 or wider, within the bound.
No kernel may reach another device: no remote copies, remote signals or barrier semaphores. Data moves between devices by JAX's collectives and lax.ppermute only.
A program may use at most 128 MiB of HBM per device.

```python
import math
import jax
import jax.numpy as jnp
from jax import lax

D = 12288
FF = 24576
TOKENS = 1024
N_ROW = 16
N_COL = 8


def steps_of(own_key, extent, shards, smallest, high):
    def one(position, shards_of):
        heights = jax.random.uniform(jax.random.fold_in(jax.random.fold_in(own_key, 6), position), (shards_of,), jnp.float32, smallest / len(shards), high / len(shards))
        return jnp.repeat(jnp.exp(heights), extent[position] // shards_of).reshape((-1,) + (1,) * (len(extent) - position - 1))

    loudness = one(*shards[0])
    for cut in shards[1:]:
        loudness = loudness * one(*cut)
    return loudness


def gaussian(key, extent, spread, reach, split=(), held_as=jnp.bfloat16):
    entries = jax.random.normal(key, extent, jnp.float32) * spread
    if len(split) > 0:
        entries = steps_of(key, extent, split, -0.22, 0.18) * entries
    return jnp.clip(entries, min=-reach, max=reach).astype(held_as)


def setup_inputs(seed: int = 0) -> dict:
    arg_keys = jax.random.split(jax.random.key(seed), 6)
    tokens = gaussian(arg_keys[0], (TOKENS, D), 1.0, 6.0, ((0, 8), (1, 16)))
    weight_in = gaussian(arg_keys[1], (D, FF), D ** -0.5, 0.0546875, ((0, 16), (1, 8)))
    weight_out = gaussian(arg_keys[2], (FF, D), FF ** -0.5, 0.0390625, ((0, 8), (1, 16)))
    bias_in = gaussian(arg_keys[3], (FF,), 0.5, 3.0, ((0, 8),))
    cotangent = gaussian(arg_keys[4], (TOKENS, D), 1.0, 6.0, ((0, 8), (1, 16)))
    return {"tokens": tokens, "weight_in": weight_in, "weight_out": weight_out, "bias_in": bias_in, "cotangent": cotangent}


gelu_coef = math.sqrt(2.0 / math.pi)
cubic_coef = 0.044715

def gelu_tanh(values):
    inner = jnp.tanh(gelu_coef * (values + cubic_coef * values * values * values))
    return 0.5 * values * (1.0 + inner)

def gelu_slope(values):
    inner = jnp.tanh(gelu_coef * (values + cubic_coef * values * values * values))
    return 0.5 * (1.0 + inner) + 0.5 * values * (1.0 - inner * inner) * gelu_coef * (1.0 + 3.0 * cubic_coef * values * values)

def rounded(values):
    return values.astype(jnp.bfloat16).astype(jnp.float32)

def reference(tokens, weight_in, weight_out, bias_in, cotangent):
    width_part = D // N_ROW
    hidden_part = FF // N_COL
    factor = 1.0 / math.sqrt(TOKENS)
    pre_gelu = jnp.zeros((TOKENS, FF), jnp.float32)
    for number in range(N_ROW):
        offset = number * width_part
        pre_gelu = pre_gelu + rounded(jnp.dot(tokens[:, offset:offset + width_part], weight_in[offset:offset + width_part, :], preferred_element_type=jnp.float32))
    pre_gelu = pre_gelu + bias_in.astype(jnp.float32)
    hidden = gelu_tanh(pre_gelu).astype(jnp.bfloat16)
    output_sum = jnp.zeros((TOKENS, D), jnp.float32)
    for number in range(N_COL):
        offset = number * hidden_part
        output_sum = output_sum + rounded(jnp.dot(hidden[:, offset:offset + hidden_part], weight_out[offset:offset + hidden_part, :], preferred_element_type=jnp.float32))
    output = output_sum.astype(jnp.bfloat16)
    back_grad = jnp.zeros((TOKENS, FF), jnp.float32)
    for number in range(N_ROW):
        offset = number * width_part
        back_grad = back_grad + rounded(jnp.dot(cotangent[:, offset:offset + width_part], weight_out[:, offset:offset + width_part].T, preferred_element_type=jnp.float32))
    slope_grad = (back_grad * gelu_slope(pre_gelu)).astype(jnp.bfloat16)
    input_sum = jnp.zeros((TOKENS, D), jnp.float32)
    for number in range(N_COL):
        offset = number * hidden_part
        input_sum = input_sum + rounded(jnp.dot(slope_grad[:, offset:offset + hidden_part], weight_in[:, offset:offset + hidden_part].T, preferred_element_type=jnp.float32))
    grad_tokens = input_sum.astype(jnp.bfloat16)
    grad_weight_in = (jnp.dot(tokens.T, slope_grad, preferred_element_type=jnp.float32) * factor).astype(jnp.bfloat16)
    grad_weight_out = (jnp.dot(hidden.T, cotangent, preferred_element_type=jnp.float32) * factor).astype(jnp.bfloat16)
    grad_bias = lax.optimization_barrier(jnp.sum(slope_grad, axis=0, dtype=jnp.float32)) * factor
    return (output, grad_tokens, grad_weight_in, grad_weight_out, grad_bias)
```

```python
import math

import jax
import jax.numpy as jnp
from jax import lax
from jax.sharding import PartitionSpec as P

gelu_coef = math.sqrt(2.0 / math.pi)
cubic_coef = 0.044715
bf16 = jnp.bfloat16
f32 = jnp.float32


def gelu_tanh(values):
    inner = jnp.tanh(gelu_coef * (values + cubic_coef * values * values * values))
    return 0.5 * values * (1.0 + inner)


def gelu_slope(values):
    inner = jnp.tanh(gelu_coef * (values + cubic_coef * values * values * values))
    return 0.5 * (1.0 + inner) + 0.5 * values * (1.0 - inner * inner) * gelu_coef * (
        1.0 + 3.0 * cubic_coef * values * values
    )


def row_step(dz, da, dc):
    pairs = []
    for r in range(16):
        z, a, c = r // 4, (r // 2) % 2, r % 2
        pairs.append((r, ((z + dz) % 4) * 4 + ((a + da) % 2) * 2 + (c + dc) % 2))
    return lambda x: lax.ppermute(x, "row", pairs)


def col_step(dy, dh):
    pairs = []
    for k in range(8):
        y, h = k // 2, k % 2
        pairs.append((k, ((y + dy) % 4) * 2 + (h + dh) % 2))
    return lambda x: lax.ppermute(x, "col", pairs)


z_up, z_down = row_step(1, 0, 0), row_step(-1, 0, 0)
a_swap = row_step(0, 1, 0)
core_swap = row_step(0, 0, 1)
y_up, y_down = col_step(1, 0), col_step(-1, 0)
h_swap = col_step(0, 1)


def ring_scatter(terms, up, down):
    n = terms.shape[0] // 8
    wide = lambda lo, hi: terms[lo * n : hi * n].astype(f32)
    first_up = up(terms[3 * n : 5 * n])
    first_down = down(terms[5 * n : 7 * n])
    second_up = up((wide(2, 3) + first_up[n:].astype(f32)).astype(bf16))
    second_down = down((wide(7, 8) + first_down[:n].astype(f32)).astype(bf16))
    low = wide(0, 1) + second_up.astype(f32) + first_down[n:].astype(f32)
    high = wide(1, 2) + first_up[:n].astype(f32) + second_down.astype(f32)
    return low, high


def ring_gather(block, up, down):
    n = block.shape[0] // 2
    below = up(block)
    above = down(block)
    far_low = up(below[:n])
    far_high = down(above[n:])
    return [block, above, far_low, far_high, below]


def scatter_first(terms):
    low, high = ring_scatter(terms, z_up, z_down)
    return low + a_swap(high.astype(bf16)).astype(f32)


def scatter_second(terms):
    n = terms.shape[0] // 2
    summed = (terms[:n].astype(f32) + a_swap(terms[n:]).astype(f32)).astype(bf16)
    low, high = ring_scatter(summed, z_up, z_down)
    return jnp.concatenate([low, high])


def gather_first(block):
    return jnp.concatenate(
        ring_gather(jnp.concatenate([block, a_swap(block)]), z_up, z_down)
    )


def gather_second(block):
    half = jnp.concatenate(ring_gather(block, z_up, z_down))
    return jnp.concatenate([half, a_swap(half)])


def dot(left, right):
    return jnp.dot(left, right, preferred_element_type=f32)


def times_transposed(left, right):
    return lax.dot_general(left, right, (((1,), (1,)), ((), ())), preferred_element_type=f32)


def over_tokens(left, right):
    return lax.dot_general(left, right, (((0,), (0,)), ((), ())), preferred_element_type=f32)


def turned(block, z, a, sign):
    parts = block.reshape(4, 2, -1, block.shape[-1])
    parts = lax.select_n(z, *[jnp.roll(parts, -sign * i, axis=0) for i in range(4)])
    parts = jnp.where(a == 0, parts, parts[:, ::-1])
    return parts


def gather_tokens(block, z, a):
    width = block.shape[-1]
    own = turned(block, z, a, 1)
    both = jnp.stack([own, h_swap(own)], axis=2)
    below = y_up(both)
    above = y_down(both)
    far = jnp.concatenate([y_up(below[:2]), y_down(above[2:])])
    first = jnp.concatenate([both, below], axis=2).reshape(-1, width)
    second = jnp.concatenate([above, far], axis=2).swapaxes(0, 1).reshape(-1, width)
    return first, second


def scatter_tokens(first, second, z, a):
    width = first.shape[-1]
    first = first.reshape(4, 2, 2, 2, -1, width)
    second = second.reshape(2, 4, 2, 2, -1, width).swapaxes(0, 1)
    blocks = [first[:, :, 0], second[:, :, 0], second[:, :, 1], first[:, :, 1]]
    terms = jnp.concatenate([b.transpose(2, 0, 1, 3, 4).reshape(-1, width) for b in blocks])
    low, high = ring_scatter(terms, y_up, y_down)
    total = (low + h_swap(high.astype(bf16)).astype(f32)).astype(bf16)
    return turned(total, z, a, -1).reshape(-1, width)


def per_device(tokens, weight_in, weight_out, bias_in, cotangent):
    row, col = lax.axis_index("row"), lax.axis_index("col")
    z, a, core = row // 4, (row // 2) % 2, row % 2
    factor = 1.0 / math.sqrt(tokens.shape[0] * lax.axis_size("col"))
    hidden_here = weight_in.shape[1] // 2
    own_at, other_at = core * hidden_here, (1 - core) * hidden_here

    in_own = lax.dynamic_slice_in_dim(weight_in, own_at, hidden_here, 1)
    in_pair = core_swap(lax.dynamic_slice_in_dim(weight_in, other_at, hidden_here, 1))
    out_own = lax.dynamic_slice_in_dim(weight_out, own_at, hidden_here, 0)
    out_pair = core_swap(lax.dynamic_slice_in_dim(weight_out, other_at, hidden_here, 0))
    in_both = jnp.concatenate([in_own, in_pair], axis=0)
    out_both = jnp.concatenate([out_own, out_pair], axis=1)
    bias = lax.dynamic_slice_in_dim(bias_in, own_at, hidden_here, 0).astype(f32)

    token_halves = gather_tokens(tokens, z, a)
    cot_halves = gather_tokens(cotangent, z, a)
    pre_gelu = []
    for half, scatter in zip(token_halves, (scatter_first, scatter_second)):
        both = jnp.concatenate([half, core_swap(half)], axis=1)
        pre_gelu.append(scatter(dot(both, in_both).astype(bf16)) + bias)
    hidden = [
        gather(gelu_tanh(p).astype(bf16))
        for p, gather in zip(pre_gelu, (gather_first, gather_second))
    ]
    back_grad = []
    for half, scatter in zip(cot_halves, (scatter_first, scatter_second)):
        both = jnp.concatenate([half, core_swap(half)], axis=1)
        back_grad.append(scatter(times_transposed(both, out_both).astype(bf16)))
    slope = [
        gather((b * gelu_slope(p)).astype(bf16))
        for b, p, gather in zip(back_grad, pre_gelu, (gather_first, gather_second))
    ]

    def summed_over_pair(own, pair):
        own, pair = own.astype(bf16), pair.astype(bf16)
        return (own.astype(f32) + core_swap(pair).astype(f32)).astype(bf16)

    output = scatter_tokens(
        *[summed_over_pair(dot(p, out_own), dot(p, out_pair)) for p in hidden], z, a
    )
    grad_tokens = scatter_tokens(
        *[
            summed_over_pair(times_transposed(p, in_own), times_transposed(p, in_pair))
            for p in slope
        ],
        z,
        a,
    )

    def all_hidden(halves):
        own = jnp.concatenate(halves)
        pair = core_swap(own)
        return jnp.where(
            core == 0,
            jnp.concatenate([own, pair], axis=1),
            jnp.concatenate([pair, own], axis=1),
        )

    hidden_all, slope_all = all_hidden(hidden), all_hidden(slope)
    tokens_all, cot_all = jnp.concatenate(token_halves), jnp.concatenate(cot_halves)
    grad_weight_out = (over_tokens(hidden_all, cot_all) * factor).astype(bf16)
    grad_weight_in = (over_tokens(tokens_all, slope_all) * factor).astype(bf16)
    grad_bias = jnp.sum(slope_all, axis=0, dtype=f32) * factor
    return (output, grad_tokens, grad_weight_in, grad_weight_out, grad_bias)


def solution(mesh):
    placed = (P("col", "row"), P("row", "col"), P("col", "row"), P("col"), P("col", "row"))
    return jax.shard_map(
        per_device,
        mesh=mesh,
        in_specs=placed,
        out_specs=(P("col", "row"), P("col", "row"), P("row", "col"), P("col", "row"), P("col")),
        check_vma=False,
    )
```

```python
import functools
import math

import jax
import jax.numpy as jnp
from jax import lax
from jax.experimental import pallas as pl
from jax.experimental.pallas import tpu as pltpu
from jax.sharding import PartitionSpec as P

gelu_coef = math.sqrt(2.0 / math.pi)
cubic_coef = 0.044715
bf16 = jnp.bfloat16
f32 = jnp.float32


def gelu_tanh(values):
    inner = jnp.tanh(gelu_coef * (values + cubic_coef * values * values * values))
    return 0.5 * values * (1.0 + inner)


def gelu_slope(values):
    inner = jnp.tanh(gelu_coef * (values + cubic_coef * values * values * values))
    return 0.5 * (1.0 + inner) + 0.5 * values * (1.0 - inner * inner) * gelu_coef * (
        1.0 + 3.0 * cubic_coef * values * values
    )


def row_step(dz, da, dc):
    pairs = []
    for r in range(16):
        z, a, c = r // 4, (r // 2) % 2, r % 2
        pairs.append((r, ((z + dz) % 4) * 4 + ((a + da) % 2) * 2 + (c + dc) % 2))
    return lambda x: lax.ppermute(x, "row", pairs)


def col_step(dy, dh):
    pairs = []
    for k in range(8):
        y, h = k // 2, k % 2
        pairs.append((k, ((y + dy) % 4) * 2 + (h + dh) % 2))
    return lambda x: lax.ppermute(x, "col", pairs)


z_up, z_down = row_step(1, 0, 0), row_step(-1, 0, 0)
a_swap = row_step(0, 1, 0)
core_swap = row_step(0, 0, 1)
y_up, y_down = col_step(1, 0), col_step(-1, 0)
y_two = col_step(2, 0)
h_swap = col_step(0, 1)


def after(value, *others):
    return lax.optimization_barrier((value,) + others)[0]


def wide(part):
    return part.astype(f32)


class Order:
    def __init__(self):
        self.last = ()

    def __call__(self, *values):
        done = lax.optimization_barrier(tuple(values) + self.last)[: len(values)]
        self.last = (min(done, key=lambda v: v.size),)
        return done if len(values) > 1 else done[0]


def scatter_start(blocks, up, down):
    m = blocks[0].shape[0] // 2
    return (
        up(jnp.concatenate([blocks[1][m:], blocks[2][:m]])),
        down(jnp.concatenate([blocks[2][m:], blocks[3][:m]])),
    )


def scatter_pass(blocks, first, up, down):
    m = blocks[0].shape[0] // 2
    return (
        up((wide(blocks[1][:m]) + wide(first[0][m:])).astype(bf16)),
        down((wide(blocks[3][m:]) + wide(first[1][:m])).astype(bf16)),
    )


def scatter_end(blocks, first, second):
    m = blocks[0].shape[0] // 2
    low = wide(blocks[0][:m]) + wide(second[0]) + wide(first[1][m:])
    high = wide(blocks[0][m:]) + wide(first[0][:m]) + wide(second[1])
    return jnp.concatenate([low, high]).astype(bf16)


def y_gather(shard):
    return [shard, y_down(shard), y_two(shard), y_up(shard)]


def y_scatter(shards):
    return [y_up(shards[1]), y_two(shards[2]), y_down(shards[3])]


def dot(left, right):
    return jnp.dot(left, right, preferred_element_type=f32)


def times_transposed(left, right):
    return lax.dot_general(left, right, (((1,), (1,)), ((), ())), preferred_element_type=f32)


def over_tokens(left, right):
    return lax.dot_general(left, right, (((0,), (0,)), ((), ())), preferred_element_type=f32)


def grad_in_kernel(factor, core, rows, own, pair, out, bias):
    def tile(part):
        for at in range(0, out.shape[0], 256):
            total = over_tokens(rows[:, at : at + 256], part[...])
            out[at : at + 256, :] = (total * factor).astype(bf16)
        bias[...] = jnp.sum(wide(part[...]), axis=0, keepdims=True) * factor

    first = pl.program_id(0) < pl.num_programs(0) // 2
    pl.when(first)(lambda: tile(own))
    pl.when(jnp.logical_not(first))(lambda: tile(pair))


def grad_out_kernel(factor, core, rows, own, pair, out):
    def tile(part):
        for at in range(0, out.shape[0], 256):
            total = over_tokens(part[:, at : at + 256], rows[...])
            out[at : at + 256, :] = (total * factor).astype(bf16)

    first = pl.program_id(0) < pl.num_programs(0) // 2
    pl.when(first)(lambda: tile(own))
    pl.when(jnp.logical_not(first))(lambda: tile(pair))


def weight_grad(core, rows, own, pair, factor, hidden_first):
    tokens, width = rows.shape
    hidden = own.shape[1]
    tile = hidden // 2
    whole = pl.BlockSpec((tokens, width), lambda i, c: (0, 0))
    from_own = pl.BlockSpec((tokens, tile), lambda i, c: (0, jnp.minimum(i, 1)))
    from_pair = pl.BlockSpec((tokens, tile), lambda i, c: (0, jnp.maximum(i - 2, 0)))
    place = lambda i, c: lax.rem(c[0] * 2 + i, 4)
    if hidden_first:
        body = grad_out_kernel
        out_specs = pl.BlockSpec((tile, width), lambda i, c: (place(i, c), 0))
        out_shape = jax.ShapeDtypeStruct((2 * hidden, width), bf16)
    else:
        body = grad_in_kernel
        out_specs = [
            pl.BlockSpec((width, tile), lambda i, c: (0, place(i, c))),
            pl.BlockSpec((1, tile), lambda i, c: (0, place(i, c))),
        ]
        out_shape = [
            jax.ShapeDtypeStruct((width, 2 * hidden), bf16),
            jax.ShapeDtypeStruct((1, 2 * hidden), f32),
        ]
    return pl.pallas_call(
        functools.partial(body, factor),
        grid_spec=pltpu.PrefetchScalarGridSpec(
            num_scalar_prefetch=1,
            grid=(4,),
            in_specs=[whole, from_own, from_pair],
            out_specs=out_specs,
        ),
        out_shape=out_shape,
        compiler_params=pltpu.CompilerParams(vmem_limit_bytes=24 << 20),
        cost_estimate=pl.CostEstimate(
            flops=4 * tokens * width * hidden,
            bytes_accessed=2 * (tokens * (width + 2 * hidden) + 2 * width * hidden),
            transcendentals=0,
        ),
        name="grad_out" if hidden_first else "grad_in",
    )(core.reshape(1).astype(jnp.int32), rows, own, pair)


def turned(block, z, sign):
    parts = block.reshape(4, -1, block.shape[-1])
    parts = jnp.concatenate([parts, parts])
    parts = lax.dynamic_slice_in_dim(parts, z if sign > 0 else 4 - z, 4, 0)
    return parts.reshape(block.shape)


def shards_to_rows(shards):
    width = shards[0].shape[-1]
    return jnp.stack([s.reshape(4, -1, width) for s in shards], axis=1).reshape(-1, width)


def rows_to_shards(rows, count):
    width = rows.shape[-1]
    return rows.reshape(4, count, -1, width).swapaxes(0, 1).reshape(count, -1, width)


def per_device(tokens, weight_in, weight_out, bias_in, cotangent):
    row = lax.axis_index("row")
    z, core = row // 4, row % 2
    factor = 1.0 / math.sqrt(tokens.shape[0] * lax.axis_size("col"))
    hidden_here = weight_in.shape[1] // 2
    own_at, other_at = core * hidden_here, (1 - core) * hidden_here

    order = Order()

    in_send = lax.dynamic_slice_in_dim(weight_in, other_at, hidden_here, 1)
    in_pair = core_swap(in_send)
    tok = turned(after(tokens, in_send), z, 1)
    near = y_gather(tok)
    *near_rest, tok_swapped = order(*near[1:], h_swap(tok))
    near = [tok, *near_rest]
    other = y_gather(tok_swapped)
    cot = turned(after(cotangent, tok_swapped), z, 1)
    cot_swapped = h_swap(cot)
    near_pair = core_swap(jnp.concatenate(near))
    in_own = lax.dynamic_slice_in_dim(after(weight_in, tok_swapped), own_at, hidden_here, 1)
    near_pair, in_pair, in_own, *other_rest = order(near_pair, in_pair, in_own, *other[1:])
    other = [tok_swapped, *other_rest]
    other_pair = core_swap(jnp.concatenate(other))
    cot_shards = y_gather(jnp.concatenate([after(cot, other[1]), after(cot_swapped, other[1])]))
    in_both = jnp.concatenate([in_own, in_pair], axis=0)
    bias = lax.dynamic_slice_in_dim(bias_in, own_at, hidden_here, 0).astype(f32)
    tok_all = shards_to_rows(near + other)
    other_pair, in_both, tok_all = order(other_pair, in_both, tok_all)

    pair_all = shards_to_rows(jnp.split(near_pair, 4) + jnp.split(other_pair, 4))
    both = order(jnp.concatenate([tok_all, pair_all], axis=1))
    terms = jnp.split(order(dot(both, in_both).astype(bf16)), 4)
    first = scatter_start(terms, z_up, z_down)
    weight_out_here = after(weight_out, terms[0])
    out_own = lax.dynamic_slice_in_dim(weight_out_here, own_at, hidden_here, 0)
    out_pair = core_swap(lax.dynamic_slice_in_dim(weight_out_here, other_at, hidden_here, 0))
    *first, cot_1, cot_2, cot_3 = order(*first, *cot_shards[1:])
    second = scatter_pass(terms, first, z_up, z_down)
    cot_shards = [cot_shards[0], cot_1, cot_2, cot_3]
    n = tokens.shape[0]
    cot_all = shards_to_rows([c[:n] for c in cot_shards] + [c[n:] for c in cot_shards])
    cot_pair, out_pair = order(core_swap(cot_all), out_pair)
    cot_wide, out_both = order(
        jnp.concatenate([cot_all, cot_pair], axis=1),
        jnp.concatenate([out_own, out_pair], axis=1),
    )

    back_terms = order(times_transposed(cot_wide, out_both).astype(bf16))
    second = order(*second)
    pre_here = scatter_end(terms, first, second)
    pre_there = a_swap(pre_here)
    terms = jnp.split(back_terms, 4)
    first = scatter_start(terms, z_up, z_down)
    *first, pre_there = order(*first, pre_there)
    second = scatter_pass(terms, first, z_up, z_down)
    pre_gelu = wide(pre_here) + wide(pre_there) + bias
    hidden_own = gelu_tanh(pre_gelu).astype(bf16)
    slope_here = gelu_slope(pre_gelu)
    *second, hidden_own, slope_here = order(*second, hidden_own, slope_here)
    back_here = scatter_end(terms, first, second)
    back_there = a_swap(back_here)

    n = hidden_own.shape[0] // 2
    first = [z_up(hidden_own), z_down(hidden_own)]
    first_up, first_down, back_there = order(*first, back_there)
    slope_own = ((wide(back_here) + wide(back_there)) * slope_here).astype(bf16)
    slope_near, slope_other = slope_own[:n], slope_own[n:]
    second_up = z_up(jnp.concatenate([first_up[:n], slope_other]))
    second_down = z_down(jnp.concatenate([first_down[n:], slope_other]))
    second_up, second_down = order(second_up, second_down)
    m = n // 2
    other_up, other_down = second_up[n:], second_down[n:]
    third_up = z_up(jnp.concatenate([other_up[:m], slope_near]))
    third_down = z_down(jnp.concatenate([other_down[m:], slope_near]))

    def summed_over_pair(terms, pair, count):
        return rows_to_shards((wide(terms[:, :width]) + wide(pair)).astype(bf16), count)

    hidden_all = jnp.concatenate(
        [hidden_own, first_down, second_up[:n], second_down[:n], first_up]
    )
    out_terms = dot(hidden_all, out_both).astype(bf16)
    out_terms, third_up, third_down = order(out_terms, third_up, third_down)
    width = out_terms.shape[1] // 2
    near_up, near_down = third_up[m:], third_down[m:]
    fourth = [z_up(near_up[:m]), z_down(near_down[m:])]
    pair = core_swap(out_terms[:, width:])
    hidden_pair = core_swap(after(hidden_all, third_up))
    slope_other = jnp.concatenate(
        [slope_other, other_down, third_up[:m], third_down[:m], other_up]
    )
    terms = times_transposed(slope_other, in_both).astype(bf16)
    terms, fourth_up, fourth_down, pair = order(terms, *fourth, pair)
    shards = summed_over_pair(out_terms, pair, 8)
    out_shards = [jnp.concatenate([shards[d], shards[4 + d]]) for d in range(4)]
    out_from = y_scatter(out_shards)
    pair = core_swap(terms[:, width:])

    slope_near = jnp.concatenate([slope_near, near_down, fourth_up, fourth_down, near_up])
    terms_near = times_transposed(slope_near, in_both).astype(bf16)
    terms_near, pair = order(terms_near, pair)
    shards_other = summed_over_pair(terms, pair, 4)
    from_other = y_scatter(shards_other)
    pair = core_swap(terms_near[:, width:])
    halves = [s.reshape(4, n, -1) for s in (slope_near, slope_other)]
    slope_all = jnp.stack(halves, axis=1).reshape(hidden_all.shape)
    slope_all, pair, hidden_pair = order(slope_all, pair, hidden_pair)
    slope_pair = core_swap(slope_all)
    shards_near = summed_over_pair(terms_near, pair, 4)
    from_near = y_scatter(shards_near)
    grad_weight_out = weight_grad(core, cot_all, hidden_all, hidden_pair, factor, True)
    grad_weight_out, *come = order(grad_weight_out, *out_from, *from_other)
    out_from, from_other = come[:3], come[3:]
    total = wide(out_shards[0]) + sum(wide(f) for f in out_from)
    k = total.shape[0] // 2
    out_here, out_there = total[:k], h_swap(total[k:].astype(bf16))
    total = wide(shards_other[0]) + sum(wide(f) for f in from_other)
    grad_there = h_swap(total.astype(bf16))
    grad_weight_in, grad_bias = weight_grad(
        core, tok_all, slope_all, slope_pair, factor, False
    )
    grad_weight_in, grad_bias, *from_near, grad_there, out_there = order(
        grad_weight_in, grad_bias, *from_near, grad_there, out_there
    )
    output = turned((out_here + wide(out_there)).astype(bf16), z, -1)
    total = wide(shards_near[0]) + sum(wide(f) for f in from_near) + wide(grad_there)
    grad_tokens = turned(total.astype(bf16), z, -1)
    return (output, grad_tokens, grad_weight_in, grad_weight_out, grad_bias.reshape(-1))


def solution(mesh):
    placed = (P("col", "row"), P("row", "col"), P("col", "row"), P("col"), P("col", "row"))
    return jax.shard_map(
        per_device,
        mesh=mesh,
        in_specs=placed,
        out_specs=(P("col", "row"), P("col", "row"), P("row", "col"), P("col", "row"), P("col")),
        check_vma=False,
    )
```

```python
import functools
import math

import jax
import jax.numpy as jnp
from jax import lax
from jax.experimental import pallas as pl
from jax.experimental.pallas import tpu as pltpu
from jax.sharding import PartitionSpec as P

gelu_coef = math.sqrt(2.0 / math.pi)
cubic_coef = 0.044715
bf16 = jnp.bfloat16
f32 = jnp.float32


def gelu_tanh(values):
    inner = jnp.tanh(gelu_coef * (values + cubic_coef * values * values * values))
    return 0.5 * values * (1.0 + inner)


def gelu_slope(values):
    inner = jnp.tanh(gelu_coef * (values + cubic_coef * values * values * values))
    return 0.5 * (1.0 + inner) + 0.5 * values * (1.0 - inner * inner) * gelu_coef * (
        1.0 + 3.0 * cubic_coef * values * values
    )


def row_step(dz, da, dc):
    pairs = []
    for r in range(16):
        z, a, c = r // 4, (r // 2) % 2, r % 2
        pairs.append((r, ((z + dz) % 4) * 4 + ((a + da) % 2) * 2 + (c + dc) % 2))
    return lambda x: lax.ppermute(x, "row", pairs)


def col_step(dy, dh):
    pairs = []
    for k in range(8):
        y, h = k // 2, k % 2
        pairs.append((k, ((y + dy) % 4) * 2 + (h + dh) % 2))
    return lambda x: lax.ppermute(x, "col", pairs)


z_up, z_down = row_step(1, 0, 0), row_step(-1, 0, 0)
a_swap = row_step(0, 1, 0)
core_swap = row_step(0, 0, 1)
y_up, y_down = col_step(1, 0), col_step(-1, 0)
y_two = col_step(2, 0)
h_swap = col_step(0, 1)


def after(value, *others):
    return lax.optimization_barrier((value,) + others)[0]


def wide(part):
    return part.astype(f32)


class Order:
    def __init__(self):
        self.last = ()

    def __call__(self, *values):
        done = lax.optimization_barrier(tuple(values) + self.last)[: len(values)]
        self.last = (min(done, key=lambda v: v.size),)
        return done if len(values) > 1 else done[0]


def scatter_start(blocks, up, down):
    m = blocks[0].shape[0] // 2
    return (
        up(jnp.concatenate([blocks[1][m:], blocks[2][:m]])),
        down(jnp.concatenate([blocks[2][m:], blocks[3][:m]])),
    )


def scatter_pass(blocks, first, up, down):
    m = blocks[0].shape[0] // 2
    return (
        up((wide(blocks[1][:m]) + wide(first[0][m:])).astype(bf16)),
        down((wide(blocks[3][m:]) + wide(first[1][:m])).astype(bf16)),
    )


def scatter_end(blocks, first, second):
    m = blocks[0].shape[0] // 2
    low = wide(blocks[0][:m]) + wide(second[0]) + wide(first[1][m:])
    high = wide(blocks[0][m:]) + wide(first[0][:m]) + wide(second[1])
    return jnp.concatenate([low, high]).astype(bf16)


def y_gather(shard):
    return [shard, y_down(shard), y_two(shard), y_up(shard)]


def y_scatter(shards):
    return [y_up(shards[1]), y_two(shards[2]), y_down(shards[3])]


def dot(left, right):
    return jnp.dot(left, right, preferred_element_type=f32)


def times_transposed(left, right):
    return lax.dot_general(left, right, (((1,), (1,)), ((), ())), preferred_element_type=f32)


def over_tokens(left, right):
    return lax.dot_general(left, right, (((0,), (0,)), ((), ())), preferred_element_type=f32)


def grad_in_kernel(factor, core, rows, own, pair, out, bias):
    def tile(part):
        for at in range(0, out.shape[0], 256):
            total = over_tokens(rows[:, at : at + 256], part[...])
            out[at : at + 256, :] = (total * factor).astype(bf16)
        bias[...] = jnp.sum(wide(part[...]), axis=0, keepdims=True) * factor

    first = pl.program_id(0) < pl.num_programs(0) // 2
    pl.when(first)(lambda: tile(own))
    pl.when(jnp.logical_not(first))(lambda: tile(pair))


def grad_out_kernel(factor, core, rows, own, pair, out):
    def tile(part):
        for at in range(0, out.shape[0], 256):
            total = over_tokens(part[:, at : at + 256], rows[...])
            out[at : at + 256, :] = (total * factor).astype(bf16)

    first = pl.program_id(0) < pl.num_programs(0) // 2
    pl.when(first)(lambda: tile(own))
    pl.when(jnp.logical_not(first))(lambda: tile(pair))


def weight_grad(core, rows, own, pair, factor, hidden_first):
    tokens, width = rows.shape
    hidden = own.shape[1]
    tile = hidden // 2
    whole = pl.BlockSpec((tokens, width), lambda i, c: (0, 0))
    from_own = pl.BlockSpec((tokens, tile), lambda i, c: (0, jnp.minimum(i, 1)))
    from_pair = pl.BlockSpec((tokens, tile), lambda i, c: (0, jnp.maximum(i - 2, 0)))
    place = lambda i, c: lax.rem(c[0] * 2 + i, 4)
    if hidden_first:
        body = grad_out_kernel
        out_specs = pl.BlockSpec((tile, width), lambda i, c: (place(i, c), 0))
        out_shape = jax.ShapeDtypeStruct((2 * hidden, width), bf16)
    else:
        body = grad_in_kernel
        out_specs = [
            pl.BlockSpec((width, tile), lambda i, c: (0, place(i, c))),
            pl.BlockSpec((1, tile), lambda i, c: (0, place(i, c))),
        ]
        out_shape = [
            jax.ShapeDtypeStruct((width, 2 * hidden), bf16),
            jax.ShapeDtypeStruct((1, 2 * hidden), f32),
        ]
    return pl.pallas_call(
        functools.partial(body, factor),
        grid_spec=pltpu.PrefetchScalarGridSpec(
            num_scalar_prefetch=1,
            grid=(4,),
            in_specs=[whole, from_own, from_pair],
            out_specs=out_specs,
        ),
        out_shape=out_shape,
        compiler_params=pltpu.CompilerParams(vmem_limit_bytes=24 << 20),
        name="grad_out" if hidden_first else "grad_in",
    )(core.reshape(1).astype(jnp.int32), rows, own, pair)


def turned(block, z, sign):
    parts = block.reshape(4, -1, block.shape[-1])
    parts = jnp.concatenate([parts, parts])
    parts = lax.dynamic_slice_in_dim(parts, z if sign > 0 else 4 - z, 4, 0)
    return parts.reshape(block.shape)


def shards_to_rows(shards):
    width = shards[0].shape[-1]
    return jnp.stack([s.reshape(4, -1, width) for s in shards], axis=1).reshape(-1, width)


def rows_to_shards(rows, count):
    width = rows.shape[-1]
    return rows.reshape(4, count, -1, width).swapaxes(0, 1).reshape(count, -1, width)


def per_device(tokens, weight_in, weight_out, bias_in, cotangent):
    row = lax.axis_index("row")
    z, core = row // 4, row % 2
    factor = 1.0 / math.sqrt(tokens.shape[0] * lax.axis_size("col"))
    hidden_here = weight_in.shape[1] // 2
    own_at, other_at = core * hidden_here, (1 - core) * hidden_here

    order = Order()

    tok = turned(tokens, z, 1)
    near = y_gather(tok)
    in_send = lax.dynamic_slice_in_dim(after(weight_in, tok), other_at, hidden_here, 1)
    in_send, *near_rest, tok_swapped = order(in_send, *near[1:], h_swap(tok))
    in_pair = core_swap(in_send)
    near = [tok, *near_rest]
    other = y_gather(tok_swapped)
    cot = turned(after(cotangent, tok_swapped), z, 1)
    cot_swapped = h_swap(cot)
    near_pair = core_swap(jnp.concatenate(near))
    in_own = lax.dynamic_slice_in_dim(after(weight_in, tok_swapped), own_at, hidden_here, 1)
    near_pair, in_pair, in_own, *other_rest = order(near_pair, in_pair, in_own, *other[1:])
    other = [tok_swapped, *other_rest]
    other_pair = core_swap(jnp.concatenate(other))
    cot_shards = y_gather(jnp.concatenate([after(cot, other[1]), after(cot_swapped, other[1])]))
    in_both = jnp.concatenate([in_own, in_pair], axis=0)
    bias = lax.dynamic_slice_in_dim(bias_in, own_at, hidden_here, 0).astype(f32)
    tok_all = shards_to_rows(near + other)
    other_pair, in_both, tok_all = order(other_pair, in_both, tok_all)

    pair_all = shards_to_rows(jnp.split(near_pair, 4) + jnp.split(other_pair, 4))
    both = order(jnp.concatenate([tok_all, pair_all], axis=1))
    terms = jnp.split(order(dot(both, in_both).astype(bf16)), 4)
    first = scatter_start(terms, z_up, z_down)
    weight_out_here = after(weight_out, terms[0])
    out_own = lax.dynamic_slice_in_dim(weight_out_here, own_at, hidden_here, 0)
    out_send = lax.dynamic_slice_in_dim(weight_out_here, other_at, hidden_here, 0)
    out_pair = core_swap(out_send)
    *first, cot_1, cot_2, cot_3 = order(*first, *cot_shards[1:])
    second = scatter_pass(terms, first, z_up, z_down)
    cot_shards = [cot_shards[0], cot_1, cot_2, cot_3]
    n = tokens.shape[0]
    cot_all = shards_to_rows([c[:n] for c in cot_shards] + [c[n:] for c in cot_shards])
    cot_pair, out_pair = order(core_swap(cot_all), out_pair)
    cot_wide, out_both = order(
        jnp.concatenate([cot_all, cot_pair], axis=1),
        jnp.concatenate([out_own, out_pair], axis=1),
    )

    back_terms = order(times_transposed(cot_wide, out_both).astype(bf16))
    second = order(*second)
    pre_here = scatter_end(terms, first, second)
    pre_there = a_swap(pre_here)
    terms = jnp.split(back_terms, 4)
    first = scatter_start(terms, z_up, z_down)
    *first, pre_there = order(*first, pre_there)
    second = scatter_pass(terms, first, z_up, z_down)
    pre_gelu = wide(pre_here) + wide(pre_there) + bias
    hidden_own = gelu_tanh(pre_gelu).astype(bf16)
    slope_here = gelu_slope(pre_gelu)
    *second, hidden_own, slope_here = order(*second, hidden_own, slope_here)
    back_here = scatter_end(terms, first, second)
    back_there = a_swap(back_here)

    n = hidden_own.shape[0] // 2
    first = [z_up(hidden_own), z_down(hidden_own)]
    first_up, first_down, back_there = order(*first, back_there)
    slope_own = ((wide(back_here) + wide(back_there)) * slope_here).astype(bf16)
    slope_near, slope_other = slope_own[:n], slope_own[n:]
    second_up = z_up(jnp.concatenate([first_up[:n], slope_other]))
    second_down = z_down(jnp.concatenate([first_down[n:], slope_other]))
    second_up, second_down = order(second_up, second_down)
    m = n // 2
    other_up, other_down = second_up[n:], second_down[n:]
    third_up = z_up(jnp.concatenate([other_up[:m], slope_near]))
    third_down = z_down(jnp.concatenate([other_down[m:], slope_near]))

    hidden_all = jnp.concatenate(
        [hidden_own, first_down, second_up[:n], second_down[:n], first_up]
    )
    hidden_pair = core_swap(hidden_all)
    out_terms = dot(hidden_all, out_own)
    out_terms, third_up, third_down = order(out_terms, third_up, third_down)
    near_up, near_down = third_up[m:], third_down[m:]
    fourth = [z_up(near_up[:m]), z_down(near_down[m:])]
    hidden_pair = order(hidden_pair)
    out_terms = (out_terms + dot(hidden_pair, out_send)).astype(bf16)
    shards = rows_to_shards(order(out_terms), 8)
    out_shards = [jnp.concatenate([shards[d], shards[4 + d]]) for d in range(4)]
    out_from = y_scatter(out_shards)

    def summed(terms, pair):
        return rows_to_shards((wide(terms[:, :width]) + wide(pair)).astype(bf16), 4)

    width = tokens.shape[1]
    slope_other = jnp.concatenate(
        [slope_other, other_down, third_up[:m], third_down[:m], other_up]
    )
    terms_other = times_transposed(slope_other, in_both).astype(bf16)
    terms_other, *fourth = order(terms_other, *fourth)
    pair_other = core_swap(terms_other[:, width:])
    slope_near = jnp.concatenate([slope_near, near_down, fourth[0], fourth[1], near_up])
    terms_near = times_transposed(slope_near, in_both).astype(bf16)
    terms_near, pair_other = order(terms_near, pair_other)
    pair_near = core_swap(terms_near[:, width:])
    halves = [s.reshape(4, n, -1) for s in (slope_near, slope_other)]
    slope_all = jnp.stack(halves, axis=1).reshape(hidden_all.shape)
    shards_other = h_swap(summed(terms_other, pair_other))
    slope_all, pair_near = order(slope_all, pair_near)
    slope_pair = core_swap(slope_all)
    shards_near = summed(terms_near, pair_near)
    grad_weight_out = weight_grad(core, cot_all, hidden_all, hidden_pair, factor, True)
    grad_weight_out, shards_near, slope_pair, *out_from = order(
        grad_weight_out, shards_near, slope_pair, *out_from
    )
    total = wide(out_shards[0]) + sum(wide(f) for f in out_from)
    k = total.shape[0] // 2
    out_here, out_there = total[:k], h_swap(total[k:].astype(bf16))
    shards = (wide(shards_near) + wide(order(shards_other))).astype(bf16)
    from_near = y_scatter(shards)
    grad_weight_in, grad_bias = weight_grad(
        core, tok_all, slope_all, slope_pair, factor, False
    )
    grad_weight_in, grad_bias, out_there, *from_near = order(
        grad_weight_in, grad_bias, out_there, *from_near
    )
    output = turned((out_here + wide(out_there)).astype(bf16), z, -1)
    total = wide(shards[0]) + sum(wide(f) for f in from_near)
    grad_tokens = turned(total.astype(bf16), z, -1)
    return (output, grad_tokens, grad_weight_in, grad_weight_out, grad_bias.reshape(-1))


def solution(mesh):
    placed = (P("col", "row"), P("row", "col"), P("col", "row"), P("col"), P("col", "row"))
    return jax.shard_map(
        per_device,
        mesh=mesh,
        in_specs=placed,
        out_specs=(P("col", "row"), P("col", "row"), P("row", "col"), P("col", "row"), P("col")),
        check_vma=False,
    )
```

```python
import functools
import math

import jax
import jax.numpy as jnp
from jax import lax
from jax.experimental import pallas as pl
from jax.experimental.pallas import tpu as pltpu
from jax.sharding import PartitionSpec as P

gelu_coef = math.sqrt(2.0 / math.pi)
cubic_coef = 0.044715
bf16 = jnp.bfloat16
f32 = jnp.float32


def gelu_tanh(values):
    inner = jnp.tanh(gelu_coef * (values + cubic_coef * values * values * values))
    return 0.5 * values * (1.0 + inner)


def gelu_slope(values):
    inner = jnp.tanh(gelu_coef * (values + cubic_coef * values * values * values))
    return 0.5 * (1.0 + inner) + 0.5 * values * (1.0 - inner * inner) * gelu_coef * (
        1.0 + 3.0 * cubic_coef * values * values
    )


def row_step(dz, da, dc):
    pairs = []
    for r in range(16):
        z, a, c = r // 4, (r // 2) % 2, r % 2
        pairs.append((r, ((z + dz) % 4) * 4 + ((a + da) % 2) * 2 + (c + dc) % 2))
    return lambda x: lax.ppermute(x, "row", pairs)


def col_step(dy, dh):
    pairs = []
    for k in range(8):
        y, h = k // 2, k % 2
        pairs.append((k, ((y + dy) % 4) * 2 + (h + dh) % 2))
    return lambda x: lax.ppermute(x, "col", pairs)


z_up, z_down = row_step(1, 0, 0), row_step(-1, 0, 0)
a_swap = row_step(0, 1, 0)
core_swap = row_step(0, 0, 1)
y_up, y_down = col_step(1, 0), col_step(-1, 0)
y_two = col_step(2, 0)
h_swap = col_step(0, 1)


def after(value, *others):
    return lax.optimization_barrier((value,) + others)[0]


def wide(part):
    return part.astype(f32)


class Order:
    def __init__(self):
        self.last = ()

    def __call__(self, *values):
        done = lax.optimization_barrier(tuple(values) + self.last)[: len(values)]
        self.last = (min(done, key=lambda v: v.size),)
        return done if len(values) > 1 else done[0]


def scatter_start(blocks, up, down):
    m = blocks[0].shape[0] // 2
    return (
        up(jnp.concatenate([blocks[1][m:], blocks[2][:m]])),
        down(jnp.concatenate([blocks[2][m:], blocks[3][:m]])),
    )


def scatter_pass(blocks, first, up, down):
    m = blocks[0].shape[0] // 2
    return (
        up((wide(blocks[1][:m]) + wide(first[0][m:])).astype(bf16)),
        down((wide(blocks[3][m:]) + wide(first[1][:m])).astype(bf16)),
    )


def scatter_end(blocks, first, second):
    m = blocks[0].shape[0] // 2
    low = wide(blocks[0][:m]) + wide(second[0]) + wide(first[1][m:])
    high = wide(blocks[0][m:]) + wide(first[0][:m]) + wide(second[1])
    return jnp.concatenate([low, high]).astype(bf16)


def y_gather(shard):
    return [shard, y_down(shard), y_two(shard), y_up(shard)]


def y_scatter(shards):
    return [y_up(shards[1]), y_two(shards[2]), y_down(shards[3])]


def dot(left, right):
    return jnp.dot(left, right, preferred_element_type=f32)


def times_transposed(left, right):
    return lax.dot_general(left, right, (((1,), (1,)), ((), ())), preferred_element_type=f32)


def over_tokens(left, right):
    return lax.dot_general(left, right, (((0,), (0,)), ((), ())), preferred_element_type=f32)


def grad_in_kernel(factor, core, rows, own, pair, out, bias):
    def tile(part):
        for at in range(0, out.shape[0], 256):
            total = over_tokens(rows[:, at : at + 256], part[...])
            out[at : at + 256, :] = (total * factor).astype(bf16)
        bias[...] = jnp.sum(wide(part[...]), axis=0, keepdims=True) * factor

    first = pl.program_id(0) < pl.num_programs(0) // 2
    pl.when(first)(lambda: tile(own))
    pl.when(jnp.logical_not(first))(lambda: tile(pair))


def grad_out_kernel(factor, core, rows, own, pair, out):
    def tile(part):
        for at in range(0, out.shape[0], 256):
            total = over_tokens(part[:, at : at + 256], rows[...])
            out[at : at + 256, :] = (total * factor).astype(bf16)

    first = pl.program_id(0) < pl.num_programs(0) // 2
    pl.when(first)(lambda: tile(own))
    pl.when(jnp.logical_not(first))(lambda: tile(pair))


def weight_grad(core, rows, own, pair, factor, hidden_first):
    tokens, width = rows.shape
    hidden = own.shape[1]
    tile = hidden // 2
    whole = pl.BlockSpec((tokens, width), lambda i, c: (0, 0))
    from_own = pl.BlockSpec((tokens, tile), lambda i, c: (0, jnp.minimum(i, 1)))
    from_pair = pl.BlockSpec((tokens, tile), lambda i, c: (0, jnp.maximum(i - 2, 0)))
    place = lambda i, c: lax.rem(c[0] * 2 + i, 4)
    if hidden_first:
        body = grad_out_kernel
        out_specs = pl.BlockSpec((tile, width), lambda i, c: (place(i, c), 0))
        out_shape = jax.ShapeDtypeStruct((2 * hidden, width), bf16)
    else:
        body = grad_in_kernel
        out_specs = [
            pl.BlockSpec((width, tile), lambda i, c: (0, place(i, c))),
            pl.BlockSpec((1, tile), lambda i, c: (0, place(i, c))),
        ]
        out_shape = [
            jax.ShapeDtypeStruct((width, 2 * hidden), bf16),
            jax.ShapeDtypeStruct((1, 2 * hidden), f32),
        ]
    return pl.pallas_call(
        functools.partial(body, factor),
        grid_spec=pltpu.PrefetchScalarGridSpec(
            num_scalar_prefetch=1,
            grid=(4,),
            in_specs=[whole, from_own, from_pair],
            out_specs=out_specs,
        ),
        out_shape=out_shape,
        compiler_params=pltpu.CompilerParams(vmem_limit_bytes=24 << 20),
        name="grad_out" if hidden_first else "grad_in",
    )(core.reshape(1).astype(jnp.int32), rows, own, pair)


def turned(block, z, sign):
    parts = block.reshape(4, -1, block.shape[-1])
    parts = jnp.concatenate([parts, parts])
    parts = lax.dynamic_slice_in_dim(parts, z if sign > 0 else 4 - z, 4, 0)
    return parts.reshape(block.shape)


def shards_to_rows(shards):
    width = shards[0].shape[-1]
    return jnp.stack([s.reshape(4, -1, width) for s in shards], axis=1).reshape(-1, width)


def rows_to_shards(rows, count):
    width = rows.shape[-1]
    return rows.reshape(4, count, -1, width).swapaxes(0, 1).reshape(count, -1, width)


def per_device(tokens, weight_in, weight_out, bias_in, cotangent):
    row = lax.axis_index("row")
    z, core = row // 4, row % 2
    factor = 1.0 / math.sqrt(tokens.shape[0] * lax.axis_size("col"))
    hidden_here = weight_in.shape[1] // 2
    own_at, other_at = core * hidden_here, (1 - core) * hidden_here

    order = Order()

    tok = turned(tokens, z, 1)
    near = y_gather(tok)
    in_send = lax.dynamic_slice_in_dim(after(weight_in, tok), other_at, hidden_here, 1)
    in_send, *near_rest, tok_swapped = order(in_send, *near[1:], h_swap(tok))
    in_pair = core_swap(in_send)
    near = [tok, *near_rest]
    other = y_gather(tok_swapped)
    cot = turned(after(cotangent, tok_swapped), z, 1)
    cot_swapped = h_swap(cot)
    near_pair = core_swap(jnp.concatenate(near))
    in_own = lax.dynamic_slice_in_dim(after(weight_in, tok_swapped), own_at, hidden_here, 1)
    near_pair, in_pair, in_own, *other_rest = order(near_pair, in_pair, in_own, *other[1:])
    other = [tok_swapped, *other_rest]
    other_pair = core_swap(jnp.concatenate(other))
    cot_shards = y_gather(jnp.concatenate([after(cot, other[1]), after(cot_swapped, other[1])]))
    in_both = jnp.concatenate([in_own, in_pair], axis=0)
    bias = lax.dynamic_slice_in_dim(bias_in, own_at, hidden_here, 0).astype(f32)
    tok_all = shards_to_rows(near + other)
    other_pair, in_both, tok_all = order(other_pair, in_both, tok_all)

    pair_all = shards_to_rows(jnp.split(near_pair, 4) + jnp.split(other_pair, 4))
    both = order(jnp.concatenate([tok_all, pair_all], axis=1))
    n = tokens.shape[0]
    middle = order(dot(both[3 * n : 7 * n], in_both).astype(bf16))
    first = [z_up(middle[: 2 * n]), z_down(middle[2 * n :])]
    start, end = order(
        dot(both[: 3 * n], in_both).astype(bf16), dot(both[7 * n :], in_both).astype(bf16)
    )
    weight_out_here = after(weight_out, end)
    out_own = lax.dynamic_slice_in_dim(weight_out_here, own_at, hidden_here, 0)
    out_send = lax.dynamic_slice_in_dim(weight_out_here, other_at, hidden_here, 0)
    out_pair = core_swap(out_send)
    *first, cot_1, cot_2, cot_3 = order(*first, *cot_shards[1:])
    second = [
        z_up((wide(start[2 * n :]) + wide(first[0][n:])).astype(bf16)),
        z_down((wide(end) + wide(first[1][:n])).astype(bf16)),
    ]
    cot_shards = [cot_shards[0], cot_1, cot_2, cot_3]
    cot_all = shards_to_rows([c[:n] for c in cot_shards] + [c[n:] for c in cot_shards])
    cot_pair, out_pair = order(core_swap(cot_all), out_pair)
    cot_wide, out_both = order(
        jnp.concatenate([cot_all, cot_pair], axis=1),
        jnp.concatenate([out_own, out_pair], axis=1),
    )

    back_terms = order(times_transposed(cot_wide, out_both).astype(bf16))
    second = order(*second)
    low = wide(start[:n]) + wide(second[0]) + wide(first[1][n:])
    high = wide(start[n : 2 * n]) + wide(first[0][:n]) + wide(second[1])
    pre_here = jnp.concatenate([low, high]).astype(bf16)
    pre_there = a_swap(pre_here)
    terms = jnp.split(back_terms, 4)
    first = scatter_start(terms, z_up, z_down)
    *first, pre_there = order(*first, pre_there)
    second = scatter_pass(terms, first, z_up, z_down)
    pre_gelu = wide(pre_here) + wide(pre_there) + bias
    hidden_own = gelu_tanh(pre_gelu).astype(bf16)
    slope_here = gelu_slope(pre_gelu)
    *second, hidden_own, slope_here = order(*second, hidden_own, slope_here)
    back_here = scatter_end(terms, first, second)
    back_there = a_swap(back_here)

    n = hidden_own.shape[0] // 2
    first = [z_up(hidden_own), z_down(hidden_own)]
    first_up, first_down, back_there = order(*first, back_there)
    slope_own = ((wide(back_here) + wide(back_there)) * slope_here).astype(bf16)
    slope_near, slope_other = slope_own[:n], slope_own[n:]
    second_up = z_up(jnp.concatenate([first_up[:n], slope_other]))
    second_down = z_down(jnp.concatenate([first_down[n:], slope_other]))
    second_up, second_down = order(second_up, second_down)
    m = n // 2
    other_up, other_down = second_up[n:], second_down[n:]
    third_up = z_up(jnp.concatenate([other_up[:m], slope_near]))
    third_down = z_down(jnp.concatenate([other_down[m:], slope_near]))

    hidden_all = jnp.concatenate(
        [hidden_own, first_down, second_up[:n], second_down[:n], first_up]
    )
    hidden_pair = core_swap(hidden_all)
    out_terms = dot(hidden_all, out_own)
    out_terms, third_up, third_down = order(out_terms, third_up, third_down)
    near_up, near_down = third_up[m:], third_down[m:]
    fourth = [z_up(near_up[:m]), z_down(near_down[m:])]
    hidden_pair = order(hidden_pair)
    out_terms = (out_terms + dot(hidden_pair, out_send)).astype(bf16)
    shards = rows_to_shards(order(out_terms), 8)
    out_shards = [jnp.concatenate([shards[d], shards[4 + d]]) for d in range(4)]
    out_from = y_scatter(out_shards)

    def summed(terms, pair):
        return rows_to_shards((wide(terms[:, :width]) + wide(pair)).astype(bf16), 4)

    width = tokens.shape[1]
    slope_other = jnp.concatenate(
        [slope_other, other_down, third_up[:m], third_down[:m], other_up]
    )
    terms_other = times_transposed(slope_other, in_both).astype(bf16)
    terms_other, *fourth = order(terms_other, *fourth)
    pair_other = core_swap(terms_other[:, width:])
    there_other = core_swap(slope_other)
    slope_near = jnp.concatenate([slope_near, near_down, fourth[0], fourth[1], near_up])
    terms_near = times_transposed(slope_near, in_both).astype(bf16)
    there_near = core_swap(slope_near)
    terms_near, pair_other, there_other = order(terms_near, pair_other, there_other)
    pair_near = core_swap(terms_near[:, width:])

    def all_rows(near, other):
        halves = [s.reshape(4, n, -1) for s in (near, other)]
        return jnp.stack(halves, axis=1).reshape(hidden_all.shape)

    shards_other = h_swap(summed(terms_other, pair_other))
    there_near, pair_near = order(there_near, pair_near)
    hidden_pair = after(hidden_pair, pair_near)
    slope_all = all_rows(slope_near, slope_other)
    slope_pair = all_rows(there_near, there_other)
    shards_near = summed(terms_near, pair_near)
    grad_weight_out = weight_grad(core, cot_all, hidden_all, hidden_pair, factor, True)
    grad_weight_in, grad_bias = weight_grad(
        core, tok_all, slope_all, slope_pair, factor, False
    )
    grad_weight_out, grad_weight_in, grad_bias, shards_near, shards_other, *out_from = order(
        grad_weight_out, grad_weight_in, grad_bias, shards_near, shards_other, *out_from
    )
    total = wide(out_shards[0]) + sum(wide(f) for f in out_from)
    k = total.shape[0] // 2
    out_here, out_there = total[:k], h_swap(total[k:].astype(bf16))
    shards = (wide(shards_near) + wide(shards_other)).astype(bf16)
    from_near = y_scatter(shards)
    out_there, *from_near = order(out_there, *from_near)
    output = turned((out_here + wide(out_there)).astype(bf16), z, -1)
    total = wide(shards[0]) + sum(wide(f) for f in from_near)
    grad_tokens = turned(total.astype(bf16), z, -1)
    return (output, grad_tokens, grad_weight_in, grad_weight_out, grad_bias.reshape(-1))


def solution(mesh):
    placed = (P("col", "row"), P("row", "col"), P("col", "row"), P("col"), P("col", "row"))
    return jax.shard_map(
        per_device,
        mesh=mesh,
        in_specs=placed,
        out_specs=(P("col", "row"), P("col", "row"), P("row", "col"), P("col", "row"), P("col")),
        check_vma=False,
    )
```

```python
import functools
import math

import jax
import jax.numpy as jnp
from jax import lax
from jax.experimental import pallas as pl
from jax.experimental.pallas import tpu as pltpu
from jax.sharding import PartitionSpec as P

gelu_coef = math.sqrt(2.0 / math.pi)
cubic_coef = 0.044715
bf16 = jnp.bfloat16
f32 = jnp.float32


def gelu_tanh(values):
    inner = jnp.tanh(gelu_coef * (values + cubic_coef * values * values * values))
    return 0.5 * values * (1.0 + inner)


def gelu_slope(values):
    inner = jnp.tanh(gelu_coef * (values + cubic_coef * values * values * values))
    return 0.5 * (1.0 + inner) + 0.5 * values * (1.0 - inner * inner) * gelu_coef * (
        1.0 + 3.0 * cubic_coef * values * values
    )


def row_step(dz, da, dc):
    pairs = []
    for r in range(16):
        z, a, c = r // 4, (r // 2) % 2, r % 2
        pairs.append((r, ((z + dz) % 4) * 4 + ((a + da) % 2) * 2 + (c + dc) % 2))
    return lambda x: lax.ppermute(x, "row", pairs)


def col_step(dy, dh):
    pairs = []
    for k in range(8):
        y, h = k // 2, k % 2
        pairs.append((k, ((y + dy) % 4) * 2 + (h + dh) % 2))
    return lambda x: lax.ppermute(x, "col", pairs)


z_up, z_down = row_step(1, 0, 0), row_step(-1, 0, 0)
a_swap = row_step(0, 1, 0)
core_swap = row_step(0, 0, 1)
y_up, y_down = col_step(1, 0), col_step(-1, 0)
y_two = col_step(2, 0)
h_swap = col_step(0, 1)


def after(value, *others):
    return lax.optimization_barrier((value,) + others)[0]


def wide(part):
    return part.astype(f32)


class Order:
    def __init__(self):
        self.last = ()

    def __call__(self, *values):
        done = lax.optimization_barrier(tuple(values) + self.last)[: len(values)]
        self.last = (min(done, key=lambda v: v.size),)
        return done if len(values) > 1 else done[0]


def scatter_start(blocks, up, down):
    m = blocks[0].shape[0] // 2
    return (
        up(jnp.concatenate([blocks[1][m:], blocks[2][:m]])),
        down(jnp.concatenate([blocks[2][m:], blocks[3][:m]])),
    )


def scatter_pass(blocks, first):
    m = blocks[0].shape[0] // 2
    return (
        (wide(blocks[1][:m]) + wide(first[0][m:])).astype(bf16),
        (wide(blocks[3][m:]) + wide(first[1][:m])).astype(bf16),
    )


def scatter_end(blocks, first, second):
    m = blocks[0].shape[0] // 2
    low = wide(blocks[0][:m]) + wide(second[0]) + wide(first[1][m:])
    high = wide(blocks[0][m:]) + wide(first[0][:m]) + wide(second[1])
    return jnp.concatenate([low, high]).astype(bf16)


def y_gather(shard):
    return [shard, y_down(shard), y_two(shard), y_up(shard)]


def y_scatter(shards):
    return [y_up(shards[1]), y_two(shards[2]), y_down(shards[3])]


def dot(left, right):
    return jnp.dot(left, right, preferred_element_type=f32)


def times_transposed(left, right):
    return lax.dot_general(left, right, (((1,), (1,)), ((), ())), preferred_element_type=f32)


def over_tokens(left, right):
    return lax.dot_general(left, right, (((0,), (0,)), ((), ())), preferred_element_type=f32)


def grad_in_kernel(factor, core, rows, own, pair, out, bias):
    def tile(part):
        for at in range(0, out.shape[0], 256):
            total = over_tokens(rows[:, at : at + 256], part[...])
            out[at : at + 256, :] = (total * factor).astype(bf16)
        bias[...] = jnp.sum(wide(part[...]), axis=0, keepdims=True) * factor

    first = pl.program_id(0) < pl.num_programs(0) // 2
    pl.when(first)(lambda: tile(own))
    pl.when(jnp.logical_not(first))(lambda: tile(pair))


def grad_out_kernel(factor, core, rows, own, pair, out):
    def tile(part):
        for at in range(0, out.shape[0], 256):
            total = over_tokens(part[:, at : at + 256], rows[...])
            out[at : at + 256, :] = (total * factor).astype(bf16)

    first = pl.program_id(0) < pl.num_programs(0) // 2
    pl.when(first)(lambda: tile(own))
    pl.when(jnp.logical_not(first))(lambda: tile(pair))


def weight_grad(core, rows, own, pair, factor, hidden_first):
    tokens, width = rows.shape
    hidden = own.shape[1]
    tile = hidden // 2
    whole = pl.BlockSpec((tokens, width), lambda i, c: (0, 0))
    from_own = pl.BlockSpec((tokens, tile), lambda i, c: (0, jnp.minimum(i, 1)))
    from_pair = pl.BlockSpec((tokens, tile), lambda i, c: (0, jnp.maximum(i - 2, 0)))
    place = lambda i, c: lax.rem(c[0] * 2 + i, 4)
    if hidden_first:
        body = grad_out_kernel
        out_specs = pl.BlockSpec((tile, width), lambda i, c: (place(i, c), 0))
        out_shape = jax.ShapeDtypeStruct((2 * hidden, width), bf16)
    else:
        body = grad_in_kernel
        out_specs = [
            pl.BlockSpec((width, tile), lambda i, c: (0, place(i, c))),
            pl.BlockSpec((1, tile), lambda i, c: (0, place(i, c))),
        ]
        out_shape = [
            jax.ShapeDtypeStruct((width, 2 * hidden), bf16),
            jax.ShapeDtypeStruct((1, 2 * hidden), f32),
        ]
    return pl.pallas_call(
        functools.partial(body, factor),
        grid_spec=pltpu.PrefetchScalarGridSpec(
            num_scalar_prefetch=1,
            grid=(4,),
            in_specs=[whole, from_own, from_pair],
            out_specs=out_specs,
        ),
        out_shape=out_shape,
        compiler_params=pltpu.CompilerParams(vmem_limit_bytes=24 << 20),
        name="grad_out" if hidden_first else "grad_in",
    )(core.reshape(1).astype(jnp.int32), rows, own, pair)


def turned(block, z, sign):
    parts = block.reshape(4, -1, block.shape[-1])
    parts = jnp.concatenate([parts, parts])
    parts = lax.dynamic_slice_in_dim(parts, z if sign > 0 else 4 - z, 4, 0)
    return parts.reshape(block.shape)


def shards_to_rows(shards):
    width = shards[0].shape[-1]
    return jnp.stack([s.reshape(4, -1, width) for s in shards], axis=1).reshape(-1, width)


def rows_to_shards(rows, count):
    width = rows.shape[-1]
    return rows.reshape(4, count, -1, width).swapaxes(0, 1).reshape(count, -1, width)


def per_device(tokens, weight_in, weight_out, bias_in, cotangent):
    row = lax.axis_index("row")
    z, core = row // 4, row % 2
    factor = 1.0 / math.sqrt(tokens.shape[0] * lax.axis_size("col"))
    hidden_here = weight_in.shape[1] // 2
    own_at, other_at = core * hidden_here, (1 - core) * hidden_here

    order = Order()

    tok = turned(tokens, z, 1)
    near = y_gather(tok)
    in_send = lax.dynamic_slice_in_dim(after(weight_in, tok), other_at, hidden_here, 1)
    in_send, *near_rest, tok_swapped = order(in_send, *near[1:], h_swap(tok))
    in_pair = core_swap(in_send)
    near = [tok, *near_rest]
    other = y_gather(tok_swapped)
    cot = turned(after(cotangent, tok_swapped), z, 1)
    cot_swapped = h_swap(cot)
    near_pair = core_swap(jnp.concatenate(near))
    in_own = lax.dynamic_slice_in_dim(after(weight_in, tok_swapped), own_at, hidden_here, 1)
    near_pair, in_pair, in_own, *other_rest = order(near_pair, in_pair, in_own, *other[1:])
    other = [tok_swapped, *other_rest]
    other_pair = core_swap(jnp.concatenate(other))
    cot_shards = y_gather(jnp.concatenate([after(cot, other[1]), after(cot_swapped, other[1])]))
    in_both = jnp.concatenate([in_own, in_pair], axis=0)
    bias = lax.dynamic_slice_in_dim(bias_in, own_at, hidden_here, 0).astype(f32)
    tok_all = shards_to_rows(near + other)
    other_pair, in_both, tok_all = order(other_pair, in_both, tok_all)

    pair_all = shards_to_rows(jnp.split(near_pair, 4) + jnp.split(other_pair, 4))
    both = order(jnp.concatenate([tok_all, pair_all], axis=1))
    n = tokens.shape[0]
    middle = order(dot(both[3 * n : 7 * n], in_both).astype(bf16))
    first = [z_up(middle[: 2 * n]), z_down(middle[2 * n :])]
    start = dot(both[: 3 * n], in_both).astype(bf16)
    end = dot(both[7 * n :], in_both).astype(bf16)
    weight_out_here = after(weight_out, middle)
    out_own = lax.dynamic_slice_in_dim(weight_out_here, own_at, hidden_here, 0)
    out_send = lax.dynamic_slice_in_dim(weight_out_here, other_at, hidden_here, 0)
    out_pair = core_swap(out_send)
    start, end, *first, cot_1, cot_2, cot_3 = order(start, end, *first, *cot_shards[1:])
    passed_up, passed_down = order(
        (wide(start[2 * n :]) + wide(first[0][n:])).astype(bf16),
        (wide(end) + wide(first[1][:n])).astype(bf16),
    )
    second = [z_up(passed_up), z_down(passed_down)]
    cot_shards = [cot_shards[0], cot_1, cot_2, cot_3]
    cot_all = shards_to_rows([c[:n] for c in cot_shards] + [c[n:] for c in cot_shards])
    cot_pair, out_pair = order(core_swap(cot_all), out_pair)
    cot_wide, out_both = order(
        jnp.concatenate([cot_all, cot_pair], axis=1),
        jnp.concatenate([out_own, out_pair], axis=1),
    )

    back_terms = order(times_transposed(cot_wide, out_both).astype(bf16))
    second = order(*second)
    low = wide(start[:n]) + wide(second[0]) + wide(first[1][n:])
    high = wide(start[n : 2 * n]) + wide(first[0][:n]) + wide(second[1])
    pre_here = jnp.concatenate([low, high]).astype(bf16)
    pre_there = a_swap(pre_here)
    terms = jnp.split(back_terms, 4)
    first = scatter_start(terms, z_up, z_down)
    *first, pre_there = order(*first, pre_there)
    passed_up, passed_down = order(*scatter_pass(terms, first))
    second = [z_up(passed_up), z_down(passed_down)]
    pre_gelu = wide(pre_here) + wide(pre_there) + bias
    hidden_own = gelu_tanh(pre_gelu).astype(bf16)
    slope_here = gelu_slope(pre_gelu)
    *second, hidden_own, slope_here = order(*second, hidden_own, slope_here)
    back_here = scatter_end(terms, first, second)
    back_there = a_swap(back_here)

    n = hidden_own.shape[0] // 2
    first = [z_up(hidden_own), z_down(hidden_own)]
    first_up, first_down, back_there = order(*first, back_there)
    slope_own = ((wide(back_here) + wide(back_there)) * slope_here).astype(bf16)
    slope_near, slope_other = slope_own[:n], slope_own[n:]
    second_up = z_up(jnp.concatenate([first_up[:n], slope_other]))
    second_down = z_down(jnp.concatenate([first_down[n:], slope_other]))
    second_up, second_down = order(second_up, second_down)
    m = n // 2
    other_up, other_down = second_up[n:], second_down[n:]
    third_up = z_up(jnp.concatenate([other_up[:m], slope_near]))
    third_down = z_down(jnp.concatenate([other_down[m:], slope_near]))

    hidden_all = jnp.concatenate(
        [hidden_own, first_down, second_up[:n], second_down[:n], first_up]
    )
    hidden_pair = core_swap(hidden_all)
    out_terms = dot(hidden_all, out_own)
    out_terms, third_up, third_down = order(out_terms, third_up, third_down)
    near_up, near_down = third_up[m:], third_down[m:]
    fourth = [z_up(near_up[:m]), z_down(near_down[m:])]
    hidden_pair = order(hidden_pair)
    out_terms = (out_terms + dot(hidden_pair, out_send)).astype(bf16)
    shards = rows_to_shards(order(out_terms), 8)
    out_shards = [jnp.concatenate([shards[d], shards[4 + d]]) for d in range(4)]
    out_from = y_scatter(out_shards)

    def summed(terms, pair):
        return rows_to_shards((wide(terms[:, :width]) + wide(pair)).astype(bf16), 4)

    width = tokens.shape[1]
    slope_other = jnp.concatenate(
        [slope_other, other_down, third_up[:m], third_down[:m], other_up]
    )
    terms_other = times_transposed(slope_other, in_both).astype(bf16)
    terms_other, *fourth = order(terms_other, *fourth)
    pair_other = core_swap(terms_other[:, width:])
    there_other = core_swap(slope_other)
    slope_near = jnp.concatenate([slope_near, near_down, fourth[0], fourth[1], near_up])
    terms_near = times_transposed(slope_near, in_both).astype(bf16)
    there_near = core_swap(slope_near)
    terms_near, pair_other, there_other = order(terms_near, pair_other, there_other)
    pair_near = core_swap(terms_near[:, width:])

    def all_rows(near, other):
        halves = [s.reshape(4, n, -1) for s in (near, other)]
        return jnp.stack(halves, axis=1).reshape(hidden_all.shape)

    shards_other = h_swap(summed(terms_other, pair_other))
    there_near, pair_near = order(there_near, pair_near)
    hidden_pair = after(hidden_pair, pair_near)
    slope_all = all_rows(slope_near, slope_other)
    slope_pair = all_rows(there_near, there_other)
    shards_near = summed(terms_near, pair_near)
    grad_weight_out = weight_grad(core, cot_all, hidden_all, hidden_pair, factor, True)
    grad_weight_in, grad_bias = weight_grad(
        core, tok_all, slope_all, slope_pair, factor, False
    )
    grad_weight_out, grad_weight_in, grad_bias, shards_near, shards_other, *out_from = order(
        grad_weight_out, grad_weight_in, grad_bias, shards_near, shards_other, *out_from
    )
    total = wide(out_shards[0]) + sum(wide(f) for f in out_from)
    k = total.shape[0] // 2
    out_here, out_there = total[:k], h_swap(total[k:].astype(bf16))
    shards = (wide(shards_near) + wide(shards_other)).astype(bf16)
    from_near = y_scatter(shards)
    out_there, *from_near = order(out_there, *from_near)
    output = turned((out_here + wide(out_there)).astype(bf16), z, -1)
    total = wide(shards[0]) + sum(wide(f) for f in from_near)
    grad_tokens = turned(total.astype(bf16), z, -1)
    return (output, grad_tokens, grad_weight_in, grad_weight_out, grad_bias.reshape(-1))


def solution(mesh):
    placed = (P("col", "row"), P("row", "col"), P("col", "row"), P("col"), P("col", "row"))
    return jax.shard_map(
        per_device,
        mesh=mesh,
        in_specs=placed,
        out_specs=(P("col", "row"), P("col", "row"), P("row", "col"), P("col", "row"), P("col")),
        check_vma=False,
    )
```

```python
import functools
import math

import jax
import jax.numpy as jnp
from jax import lax
from jax.experimental import pallas as pl
from jax.experimental.pallas import tpu as pltpu
from jax.sharding import PartitionSpec as P

gelu_coef = math.sqrt(2.0 / math.pi)
cubic_coef = 0.044715
bf16 = jnp.bfloat16
f32 = jnp.float32


def gelu_tanh(values):
    inner = jnp.tanh(gelu_coef * (values + cubic_coef * values * values * values))
    return 0.5 * values * (1.0 + inner)


def gelu_slope(values):
    inner = jnp.tanh(gelu_coef * (values + cubic_coef * values * values * values))
    return 0.5 * (1.0 + inner) + 0.5 * values * (1.0 - inner * inner) * gelu_coef * (
        1.0 + 3.0 * cubic_coef * values * values
    )


def row_step(dz, da, dc):
    pairs = []
    for r in range(16):
        z, a, c = r // 4, (r // 2) % 2, r % 2
        pairs.append((r, ((z + dz) % 4) * 4 + ((a + da) % 2) * 2 + (c + dc) % 2))
    return lambda x: lax.ppermute(x, "row", pairs)


def col_step(dy, dh):
    pairs = []
    for k in range(8):
        y, h = k // 2, k % 2
        pairs.append((k, ((y + dy) % 4) * 2 + (h + dh) % 2))
    return lambda x: lax.ppermute(x, "col", pairs)


z_up, z_down = row_step(1, 0, 0), row_step(-1, 0, 0)
a_swap = row_step(0, 1, 0)
core_swap = row_step(0, 0, 1)
y_up, y_down = col_step(1, 0), col_step(-1, 0)
y_two = col_step(2, 0)
h_swap = col_step(0, 1)


def after(value, *others):
    return lax.optimization_barrier((value,) + others)[0]


def wide(part):
    return part.astype(f32)


class Order:
    def __init__(self):
        self.last = ()

    def __call__(self, *values):
        done = lax.optimization_barrier(tuple(values) + self.last)[: len(values)]
        self.last = (min(done, key=lambda v: v.size),)
        return done if len(values) > 1 else done[0]


def scatter_start(blocks, up, down):
    m = blocks[0].shape[0] // 2
    return (
        up(jnp.concatenate([blocks[1][m:], blocks[2][:m]])),
        down(jnp.concatenate([blocks[2][m:], blocks[3][:m]])),
    )


def scatter_pass(blocks, first):
    m = blocks[0].shape[0] // 2
    return (
        (wide(blocks[1][:m]) + wide(first[0][m:])).astype(bf16),
        (wide(blocks[3][m:]) + wide(first[1][:m])).astype(bf16),
    )


def scatter_end(blocks, first, second):
    m = blocks[0].shape[0] // 2
    low = wide(blocks[0][:m]) + wide(second[0]) + wide(first[1][m:])
    high = wide(blocks[0][m:]) + wide(first[0][:m]) + wide(second[1])
    return jnp.concatenate([low, high]).astype(bf16)


def y_gather(shard):
    return [shard, y_down(shard), y_two(shard), y_up(shard)]


def y_scatter(shards):
    return [y_up(shards[1]), y_two(shards[2]), y_down(shards[3])]


def dot(left, right):
    return jnp.dot(left, right, preferred_element_type=f32)


def times_transposed(left, right):
    return lax.dot_general(left, right, (((1,), (1,)), ((), ())), preferred_element_type=f32)


def over_tokens(left, right):
    return lax.dot_general(left, right, (((0,), (0,)), ((), ())), preferred_element_type=f32)


def for_each_part(own, pair, width, tile):
    step = pl.program_id(0)
    at = pl.ds(pl.multiple_of(lax.rem(step, 2) * width, width), width)
    pl.when(step < 2)(lambda: tile(own.at[:, at]))
    pl.when(step >= 2)(lambda: tile(pair.at[:, at]))


def grad_in_kernel(factor, core, rows, own, pair, out, bias):
    def tile(part):
        for at in range(0, out.shape[0], 256):
            total = over_tokens(rows[:, at : at + 256], part[...])
            out[at : at + 256, :] = (total * factor).astype(bf16)
        bias[...] = jnp.sum(wide(part[...]), axis=0, keepdims=True) * factor

    for_each_part(own, pair, out.shape[1], tile)


def grad_out_kernel(factor, core, rows, own, pair, out):
    def tile(part):
        for at in range(0, out.shape[0], 256):
            total = over_tokens(part[:, at : at + 256], rows[...])
            out[at : at + 256, :] = (total * factor).astype(bf16)

    for_each_part(own, pair, out.shape[0], tile)


def weight_grad(core, rows, own, pair, factor, hidden_first):
    tokens, width = rows.shape
    hidden = own.shape[1]
    tile = hidden // 2
    whole = pl.BlockSpec(memory_space=pltpu.VMEM)
    place = lambda i, c: lax.rem(c[0] * 2 + i, 4)
    if hidden_first:
        body = grad_out_kernel
        out_specs = pl.BlockSpec((tile, width), lambda i, c: (place(i, c), 0))
        out_shape = jax.ShapeDtypeStruct((2 * hidden, width), bf16)
    else:
        body = grad_in_kernel
        out_specs = [
            pl.BlockSpec((width, tile), lambda i, c: (0, place(i, c))),
            pl.BlockSpec((1, tile), lambda i, c: (0, place(i, c))),
        ]
        out_shape = [
            jax.ShapeDtypeStruct((width, 2 * hidden), bf16),
            jax.ShapeDtypeStruct((1, 2 * hidden), f32),
        ]
    return pl.pallas_call(
        functools.partial(body, factor),
        grid_spec=pltpu.PrefetchScalarGridSpec(
            num_scalar_prefetch=1,
            grid=(4,),
            in_specs=[whole] * 3,
            out_specs=out_specs,
        ),
        out_shape=out_shape,
        compiler_params=pltpu.CompilerParams(vmem_limit_bytes=24 << 20),
        name="grad_out" if hidden_first else "grad_in",
    )(core.reshape(1).astype(jnp.int32), rows, own, pair)


def turned(block, z, sign):
    parts = block.reshape(4, -1, block.shape[-1])
    parts = jnp.concatenate([parts, parts])
    parts = lax.dynamic_slice_in_dim(parts, z if sign > 0 else 4 - z, 4, 0)
    return parts.reshape(block.shape)


def shards_to_rows(shards):
    width = shards[0].shape[-1]
    return jnp.stack([s.reshape(4, -1, width) for s in shards], axis=1).reshape(-1, width)


def rows_to_shards(rows, count):
    width = rows.shape[-1]
    return rows.reshape(4, count, -1, width).swapaxes(0, 1).reshape(count, -1, width)


def per_device(tokens, weight_in, weight_out, bias_in, cotangent):
    row = lax.axis_index("row")
    z, core = row // 4, row % 2
    factor = 1.0 / math.sqrt(tokens.shape[0] * lax.axis_size("col"))
    hidden_here = weight_in.shape[1] // 2
    own_at, other_at = core * hidden_here, (1 - core) * hidden_here

    order = Order()

    tok = turned(tokens, z, 1)
    near = y_gather(tok)
    in_send = lax.dynamic_slice_in_dim(after(weight_in, tok), other_at, hidden_here, 1)
    in_send, *near_rest, tok_swapped = order(in_send, *near[1:], h_swap(tok))
    in_pair = core_swap(in_send)
    near = [tok, *near_rest]
    other = y_gather(tok_swapped)
    cot = turned(after(cotangent, tok_swapped), z, 1)
    cot_swapped = h_swap(cot)
    near_pair = core_swap(jnp.concatenate(near))
    in_own = lax.dynamic_slice_in_dim(after(weight_in, tok_swapped), own_at, hidden_here, 1)
    near_pair, in_pair, in_own, *other_rest = order(near_pair, in_pair, in_own, *other[1:])
    other = [tok_swapped, *other_rest]
    other_pair = core_swap(jnp.concatenate(other))
    cot_shards = y_gather(jnp.concatenate([after(cot, other[1]), after(cot_swapped, other[1])]))
    in_both = jnp.concatenate([in_own, in_pair], axis=0)
    bias = lax.dynamic_slice_in_dim(bias_in, own_at, hidden_here, 0).astype(f32)
    tok_all = shards_to_rows(near + other)
    other_pair, in_both, tok_all = order(other_pair, in_both, tok_all)

    pair_all = shards_to_rows(jnp.split(near_pair, 4) + jnp.split(other_pair, 4))
    both = order(jnp.concatenate([tok_all, pair_all], axis=1))
    n = tokens.shape[0]
    middle = order(dot(both[3 * n : 7 * n], in_both).astype(bf16))
    first = [z_up(middle[: 2 * n]), z_down(middle[2 * n :])]
    start = dot(both[: 3 * n], in_both).astype(bf16)
    end = dot(both[7 * n :], in_both).astype(bf16)
    weight_out_here = after(weight_out, middle)
    out_own = lax.dynamic_slice_in_dim(weight_out_here, own_at, hidden_here, 0)
    out_send = lax.dynamic_slice_in_dim(weight_out_here, other_at, hidden_here, 0)
    out_pair = core_swap(out_send)
    start, end, *first, cot_1, cot_2, cot_3 = order(start, end, *first, *cot_shards[1:])
    passed_up, passed_down = order(
        (wide(start[2 * n :]) + wide(first[0][n:])).astype(bf16),
        (wide(end) + wide(first[1][:n])).astype(bf16),
    )
    second = [z_up(passed_up), z_down(passed_down)]
    cot_shards = [cot_shards[0], cot_1, cot_2, cot_3]
    cot_all = shards_to_rows([c[:n] for c in cot_shards] + [c[n:] for c in cot_shards])
    cot_pair, out_pair = order(core_swap(cot_all), out_pair)
    cot_wide, out_both = order(
        jnp.concatenate([cot_all, cot_pair], axis=1),
        jnp.concatenate([out_own, out_pair], axis=1),
    )

    back_terms = order(times_transposed(cot_wide, out_both).astype(bf16))
    second = order(*second)
    low = wide(start[:n]) + wide(second[0]) + wide(first[1][n:])
    high = wide(start[n : 2 * n]) + wide(first[0][:n]) + wide(second[1])
    pre_here = jnp.concatenate([low, high]).astype(bf16)
    pre_there = a_swap(pre_here)
    terms = jnp.split(back_terms, 4)
    first = scatter_start(terms, z_up, z_down)
    *first, pre_there = order(*first, pre_there)
    passed_up, passed_down = order(*scatter_pass(terms, first))
    second = [z_up(passed_up), z_down(passed_down)]
    pre_gelu = wide(pre_here) + wide(pre_there) + bias
    hidden_own = gelu_tanh(pre_gelu).astype(bf16)
    slope_here = gelu_slope(pre_gelu)
    *second, hidden_own, slope_here = order(*second, hidden_own, slope_here)
    back_here = scatter_end(terms, first, second)
    back_there = a_swap(back_here)

    n = hidden_own.shape[0] // 2
    first = [z_up(hidden_own), z_down(hidden_own)]
    first_up, first_down, back_there = order(*first, back_there)
    slope_own = ((wide(back_here) + wide(back_there)) * slope_here).astype(bf16)
    slope_near, slope_other = slope_own[:n], slope_own[n:]
    second_up = z_up(jnp.concatenate([first_up[:n], slope_other]))
    second_down = z_down(jnp.concatenate([first_down[n:], slope_other]))
    second_up, second_down = order(second_up, second_down)
    m = n // 2
    other_up, other_down = second_up[n:], second_down[n:]
    third_up = z_up(jnp.concatenate([other_up[:m], slope_near]))
    third_down = z_down(jnp.concatenate([other_down[m:], slope_near]))

    hidden_all = jnp.concatenate(
        [hidden_own, first_down, second_up[:n], second_down[:n], first_up]
    )
    hidden_pair = core_swap(hidden_all)
    out_terms = dot(hidden_all, out_own)
    out_terms, third_up, third_down = order(out_terms, third_up, third_down)
    near_up, near_down = third_up[m:], third_down[m:]
    fourth = [z_up(near_up[:m]), z_down(near_down[m:])]
    hidden_pair = order(hidden_pair)
    out_terms = (out_terms + dot(hidden_pair, out_send)).astype(bf16)
    shards = rows_to_shards(order(out_terms), 8)
    out_shards = [jnp.concatenate([shards[d], shards[4 + d]]) for d in range(4)]
    out_from = y_scatter(out_shards)

    def summed(terms, pair):
        return rows_to_shards((wide(terms[:, :width]) + wide(pair)).astype(bf16), 4)

    width = tokens.shape[1]
    slope_other = jnp.concatenate(
        [slope_other, other_down, third_up[:m], third_down[:m], other_up]
    )
    terms_other = times_transposed(slope_other, in_both).astype(bf16)
    terms_other, *fourth = order(terms_other, *fourth)
    pair_other = core_swap(terms_other[:, width:])
    there_other = core_swap(slope_other)
    slope_near = jnp.concatenate([slope_near, near_down, fourth[0], fourth[1], near_up])
    terms_near = times_transposed(slope_near, in_both).astype(bf16)
    there_near = core_swap(slope_near)
    terms_near, pair_other, there_other = order(terms_near, pair_other, there_other)
    pair_near = core_swap(terms_near[:, width:])

    def all_rows(near, other):
        halves = [s.reshape(4, n, -1) for s in (near, other)]
        return jnp.stack(halves, axis=1).reshape(hidden_all.shape)

    shards_other = h_swap(summed(terms_other, pair_other))
    there_near, pair_near = order(there_near, pair_near)
    hidden_pair = after(hidden_pair, pair_near)
    slope_all = all_rows(slope_near, slope_other)
    slope_pair = all_rows(there_near, there_other)
    shards_near = summed(terms_near, pair_near)
    grad_weight_out = weight_grad(core, cot_all, hidden_all, hidden_pair, factor, True)
    grad_weight_in, grad_bias = weight_grad(
        core, tok_all, slope_all, slope_pair, factor, False
    )
    grad_weight_out, grad_weight_in, grad_bias, shards_near, shards_other, *out_from = order(
        grad_weight_out, grad_weight_in, grad_bias, shards_near, shards_other, *out_from
    )
    total = wide(out_shards[0]) + sum(wide(f) for f in out_from)
    k = total.shape[0] // 2
    out_here, out_there = total[:k], h_swap(total[k:].astype(bf16))
    shards = (wide(shards_near) + wide(shards_other)).astype(bf16)
    from_near = y_scatter(shards)
    out_there, *from_near = order(out_there, *from_near)
    output = turned((out_here + wide(out_there)).astype(bf16), z, -1)
    total = wide(shards[0]) + sum(wide(f) for f in from_near)
    grad_tokens = turned(total.astype(bf16), z, -1)
    return (output, grad_tokens, grad_weight_in, grad_weight_out, grad_bias.reshape(-1))


def solution(mesh):
    placed = (P("col", "row"), P("row", "col"), P("col", "row"), P("col"), P("col", "row"))
    return jax.shard_map(
        per_device,
        mesh=mesh,
        in_specs=placed,
        out_specs=(P("col", "row"), P("col", "row"), P("row", "col"), P("col", "row"), P("col")),
        check_vma=False,
    )
```
